32 devices in a mesh: row: 16 (over z, y, core), col: 2 (over x).
Axes of the slice: x: 2, y: 2, z: 4, core: 2. Of those that a mesh axis runs over, the one named last changes fastest.
Arguments:
- matrix: float32 [14336, 14336], P('row', 'col'), may hold values from -16 to 16, as said below
- panels: float32 [2, 14336, 128], P(None, 'row'), may hold values from -0.050111484 to 0.050111484
- factors: float32 [2, 128, 128], replicated, may hold values from -1.2 to 1.6, as said below
Outputs:
- updated: float32 [14336, 14336], P('row', 'col')
The draws below stay inside these ranges and needn't reach their ends.
Inputs may be any that keep to these rules, and one draw needn't show every extreme that they name: symmetric: matrix[r, c] equals matrix[c, r]. Each factors[p] is upper triangular, with diagonal entries between 0.8 and 1.6.
All inputs are finite; a program needn't handle non-finite values.
Results may differ from the reference program's by a relative error of at most 0.0001.
Values sent between devices are 32-bit elements; how exact they have to be, the bound alone decides.
No kernel may reach another device: no remote copies, remote signals or barrier semaphores. Data moves between devices by JAX's collectives and lax.ppermute only.
A program may use at most 128 MiB of HBM per device.

```python
import math
import jax
import jax.numpy as jnp
from jax import lax

N = 14336
B = 128
PANELS = 2


def draw_matrix(key, part):
    inner_key = jax.random.fold_in(key, 101)
    normal_key = jax.random.fold_in(inner_key, 0)
    values = jax.random.normal(normal_key, (N, N), jnp.float32)
    values = jnp.clip(values, -4.0, 4.0)
    values = (values + values.T) * 0.5
    values = values * math.sqrt(2.0)
    values = jnp.clip(values, -4.0, 4.0)
    return values


def draw_factors(key, part):
    inner_key = jax.random.fold_in(key, 202)
    upper_key, diag_key = jax.random.split(inner_key)
    upper = jnp.clip(0.2 * jax.random.normal(upper_key, (PANELS, B, B), jnp.float32), -1.2, 1.2)
    upper = jnp.triu(upper, 1)
    diagonal = jax.random.uniform(diag_key, (PANELS, B), jnp.float32, 0.8, 1.6)
    return upper + jnp.eye(B, dtype=jnp.float32)[None, :, :] * diagonal[:, None, :]


def shard_levels(key, dims, shards, low, top_value):
    loudness = 1.0
    for position, shards_of in shards:
        draws = jax.random.uniform(jax.random.fold_in(jax.random.fold_in(key, 6), position), (shards_of,), jnp.float32, low / len(shards), top_value / len(shards))
        loudness = loudness * jnp.repeat(jnp.exp(draws), dims[position] // shards_of).reshape((-1,) + (1,) * (len(dims) - 1 - position))
    return loudness


def gaussian(stream_key, shape, deviation, limit, cuts=(), held_as=jnp.bfloat16):
    result = jax.random.normal(stream_key, shape, jnp.float32) * deviation
    if len(cuts) > 0:
        result = shard_levels(stream_key, shape, cuts, -0.22, 0.18) * result
    return jnp.clip(result, min=-limit, max=limit).astype(held_as)


def setup_inputs(seed: int = 0) -> dict:
    arg_keys = jax.random.split(jax.random.key(seed), 4)
    return {
        "matrix": draw_matrix(jax.random.fold_in(arg_keys[3], 71), 0),
        "panels": gaussian(arg_keys[1], (PANELS, N, B), (N ** -0.5), 0.050111484, ((1, 16),), jnp.float32),
        "factors": draw_factors(jax.random.fold_in(arg_keys[3], 71), 0),
    }


def reference(matrix, panels, factors):
    current = matrix
    for number in range(PANELS):
        vectors = panels[number]
        factor = factors[number]
        forward = jnp.dot(current, vectors, precision=lax.Precision.HIGHEST)
        scaled = jnp.dot(forward, factor, precision=lax.Precision.HIGHEST)
        projected = jnp.dot(vectors.T, scaled, precision=lax.Precision.HIGHEST)
        correct = jnp.dot(factor.T, projected, precision=lax.Precision.HIGHEST)
        weights = scaled - 0.5 * jnp.dot(vectors, correct, precision=lax.Precision.HIGHEST)
        current = current - jnp.dot(vectors, weights.T, precision=lax.Precision.HIGHEST)
        current = current - jnp.dot(weights, vectors.T, precision=lax.Precision.HIGHEST)
    return current
```

```python
import functools

import jax
import jax.numpy as jnp
from jax import lax
from jax.experimental import pallas as pl
from jax.experimental.pallas import tpu as pltpu
from jax.sharding import PartitionSpec as P

F32 = jnp.float32
BF16 = jnp.bfloat16
PLAIN = (((1,), (0,)), ((), ()))
BOTH_LAST = (((1,), (1,)), ((), ()))
BOTH_FIRST = (((0,), (0,)), ((), ()))
VMEM_BYTES = 48 * 1024 * 1024
STEPS = 2


def split(values):
    high = values.astype(BF16)
    return high, (values - high.astype(F32)).astype(BF16)


def product(former, latter, dims=PLAIN):
    dot = functools.partial(lax.dot_general, dimension_numbers=dims, preferred_element_type=F32)
    return dot(former[0], latter[0]) + (dot(former[0], latter[1]) + dot(former[1], latter[0]))


def small(former, latter, dims=PLAIN):
    return lax.dot_general(
        former, latter, dims, precision=lax.Precision.HIGHEST, preferred_element_type=F32
    )


def in_order(place, joined, pairs):
    odd = place[0] % 2 != 0
    depth, width = pairs[0][0].shape
    for number, (near, far) in enumerate(pairs):
        lanes = slice(number * width, (number + 1) * width)
        for top, block in ((0, jnp.where(odd, far[...], near[...])), (depth, jnp.where(odd, near[...], far[...]))):
            high, low = split(block)
            joined[0][top : top + depth, lanes] = high
            joined[1][top : top + depth, lanes] = low


def forward_kernel(first, last, place, block, *refs):
    pairs, refs, joined = (refs[:2], refs[2:4]), refs[4:-2], refs[-2:]
    step = pl.program_id(0)
    pl.when(step == 0)(lambda: in_order(place, joined, pairs))
    total = product(split(block[...]), (joined[0][...], joined[1][...]))
    if not first:
        total = total + refs[0][...]
        refs = refs[1:]
    if not last:
        refs[0][...] = total
        return
    own, kept, sent, inner = refs
    width = own.shape[2]
    one, two = total[:, :width], total[:, width:]
    swap = place[1] != 0
    kept[...] = jnp.where(swap, two, one)
    sent[...] = jnp.where(swap, one, two)

    @pl.when(step == 0)
    def _():
        inner[...] = jnp.zeros_like(inner)

    inner[0] += small(own[0], one, BOTH_FIRST)
    inner[1] += small(own[1], one, BOTH_FIRST)
    inner[2] += small(own[1], two, BOTH_FIRST)
    inner[3] += small(own[0], own[1], BOTH_FIRST)


def forward_step(place, matrix, slot, pairs, before, own):
    rows = matrix.shape[0]
    depth, width = pairs[0][0].shape
    tile = rows // STEPS
    first, last = before is None, own is not None
    whole = lambda shape: pl.BlockSpec(shape, lambda step, place: (0,) * len(shape))
    strip = lambda columns: pl.BlockSpec((tile, columns), lambda step, place: (step, 0))
    operands = [matrix, *pairs[0], *pairs[1]]
    specs = [pl.BlockSpec((tile, 2 * depth), lambda step, place: (step, (place[0] ^ slot) // 2))]
    specs += [whole((depth, width))] * 4
    if not first:
        operands.append(before)
        specs.append(strip(2 * width))
    outs, out_specs = [jax.ShapeDtypeStruct((rows, 2 * width), F32)], [strip(2 * width)]
    if last:
        operands.append(own)
        specs.append(pl.BlockSpec((2, tile, width), lambda step, place: (0, step, 0)))
        part = jax.ShapeDtypeStruct((rows, width), F32)
        outs = [part, part, jax.ShapeDtypeStruct((4, width, width), F32)]
        out_specs = [strip(width), strip(width), whole(outs[2].shape)]
    return pl.pallas_call(
        functools.partial(forward_kernel, first, last),
        grid_spec=pltpu.PrefetchScalarGridSpec(
            num_scalar_prefetch=1,
            grid=(STEPS,),
            in_specs=specs,
            out_specs=out_specs,
            scratch_shapes=[pltpu.VMEM((2 * depth, 2 * width), BF16)] * 2,
        ),
        out_shape=outs,
        compiler_params=pltpu.CompilerParams(vmem_limit_bytes=VMEM_BYTES),
        cost_estimate=pl.CostEstimate(
            flops=6 * rows * depth * 4 * width, bytes_accessed=8 * rows * depth, transcendentals=0
        ),
    )(place, *operands)


def mix_kernel(place, own, mine, other, inner, factors, high, low):
    one, two = factors[0], factors[1]
    gram_one, cross_yv, gram_old, cross_vv = inner[0], inner[1], inner[2], inner[3]
    correct_one = small(small(one, gram_one, BOTH_FIRST), one)
    cross_wv = small(one, cross_yv, (((0,), (1,)), ((), ()))) - 0.5 * small(
        correct_one, cross_vv, BOTH_FIRST
    )
    drop = small(cross_vv, cross_wv, BOTH_FIRST)
    gram_two = gram_old - drop - small(cross_wv, cross_vv, BOTH_FIRST)
    correct_two = small(small(two, gram_two, BOTH_FIRST), two)
    mixed = -small(small(one, cross_vv), two)
    edge = small(0.5 * small(correct_one, cross_vv) - cross_wv, two)
    swap = place[1] != 0
    y_one = jnp.where(swap, other[...], mine[...])
    y_two = jnp.where(swap, mine[...], other[...])
    v_one, v_two = own[0], own[1]
    p_one = small(v_one, one, BOTH_LAST) + small(v_two, mixed, BOTH_LAST)
    p_two = small(v_two, two, BOTH_LAST)
    q_one = (
        small(y_one, one)
        - small(v_one, 0.5 * (correct_one + correct_one.T))
        + small(v_two, edge, BOTH_LAST)
    )
    q_two = (
        small(y_one, mixed)
        + small(y_two, two)
        + small(v_one, edge)
        - small(v_two, 0.5 * (correct_two + correct_two.T))
    )
    turn = place[2] != 0
    parts = (jnp.where(turn, p_two, p_one), jnp.where(turn, p_one, p_two), q_one, q_two)
    width = v_one.shape[1]
    for number, part in enumerate(parts):
        lanes = slice(number * width, (number + 1) * width)
        high[:, lanes], low[:, lanes] = split(part)


def mix(place, own, mine, other, inner, factors):
    rows, width = mine.shape
    side = jax.ShapeDtypeStruct((rows, 4 * width), BF16)
    vmem = pl.BlockSpec(memory_space=pltpu.VMEM)
    return pl.pallas_call(
        mix_kernel,
        in_specs=[pl.BlockSpec(memory_space=pltpu.SMEM)] + [vmem] * 5,
        out_specs=[vmem, vmem],
        out_shape=[side, side],
        compiler_params=pltpu.CompilerParams(vmem_limit_bytes=VMEM_BYTES),
        cost_estimate=pl.CostEstimate(
            flops=12 * rows * width * 8 * width, bytes_accessed=32 * rows * width, transcendentals=0
        ),
    )(place, own, mine, other, inner, factors)


def update_kernel(first, place, block, high, low, *refs):
    pairs, out, joined = [refs[2 * n : 2 * n + 2] for n in range(4)], refs[-3], refs[-2:]
    pl.when(pl.program_id(0) == 0)(lambda: in_order(place, joined, pairs))
    side = (joined[0][...], joined[1][...])
    out[...] = block[...] - product((high[...], low[...]), side, BOTH_LAST)


def update_step(place, matrix, slot, sides, pairs, before):
    rows = matrix.shape[0]
    depth, width = pairs[0][0].shape
    tile = rows // STEPS
    first = before is None
    block = pl.BlockSpec((tile, 2 * depth), lambda step, place: (step, (place[0] ^ slot) // 2))
    strip = pl.BlockSpec((tile, 4 * width), lambda step, place: (step, 0))
    whole = pl.BlockSpec((depth, width), lambda step, place: (0, 0))
    operands = [matrix, *sides] + [part for pair in pairs for part in pair]
    specs = [block, strip, strip] + [whole] * 8
    aliases = {}
    if not first:
        aliases = {1 + len(operands): 0}
        operands.append(before)
        specs.append(pl.BlockSpec(memory_space=pl.ANY))
    return pl.pallas_call(
        functools.partial(update_kernel, first),
        grid_spec=pltpu.PrefetchScalarGridSpec(
            num_scalar_prefetch=1,
            grid=(STEPS,),
            in_specs=specs,
            out_specs=block,
            scratch_shapes=[pltpu.VMEM((2 * depth, 4 * width), BF16)] * 2,
        ),
        out_shape=jax.ShapeDtypeStruct(matrix.shape, F32),
        input_output_aliases=aliases,
        compiler_params=pltpu.CompilerParams(vmem_limit_bytes=VMEM_BYTES),
        cost_estimate=pl.CostEstimate(
            flops=6 * rows * depth * 8 * width, bytes_accessed=16 * rows * depth, transcendentals=0
        ),
    )(place, *operands)


def solution(mesh):
    row_count, col_count = mesh.shape["row"], mesh.shape["col"]
    group = row_count // col_count
    assert group * col_count == row_count and group >= 2 and group & (group - 1) == 0
    halves = col_count == 2

    def flip(values, axis, bit):
        count = mesh.shape[axis]
        return lax.ppermute(values, axis, [(i, i ^ bit) for i in range(count)])

    def transpose(values, turn):
        pairs = []
        for s in range(col_count):
            for b in range(group):
                for j in range(col_count):
                    source = (s * group + b) * col_count + j
                    pairs.append((source, ((j - turn) % col_count * group + b) * col_count + s))
        return lax.ppermute(values, ("row", "col"), pairs)

    def spread(own):
        found = {0: own}
        for d in range(2, group, 2):
            found[d] = flip(own, "row", d)
        for d in range(0, group, 2):
            found[d + 1] = flip(found[d], "row", 1)
        return found

    def total(values):
        for axis in ("col", "row"):
            count = mesh.shape[axis]
            if count & (count - 1):
                values = lax.psum(values, axis)
                continue
            bit = 1
            while bit < count:
                values = values + flip(values, axis, bit)
                bit *= 2
        return values

    def shards(matrix, panels, factors):
        row, col = lax.axis_index("row"), lax.axis_index("col")
        zero = jnp.zeros_like(row)
        place = jnp.stack(
            [row % group, col if halves else zero, row // group if halves else zero]
        ).astype(jnp.int32)
        vectors = [spread(transpose(panels[p], p)) for p in range(2)]
        partial = None
        for slot in range(0, group, 2):
            pairs = [(v[slot], v[slot + 1]) for v in vectors]
            last = slot + 2 == group
            found = forward_step(place, matrix, slot, pairs, partial, panels if last else None)
            partial = found[0]
        kept, sent, inner = found
        inner = total(inner * jnp.array([1, 1, 1, 1 / col_count], F32)[:, None, None])
        if halves:
            mine = kept + flip(sent, "col", 1)
            other = flip(mine, "col", 1)
            firsts, seconds = transpose(mine, 0), transpose(mine, 1)
        else:
            mine, other = lax.psum((kept, sent), "col")
            firsts, seconds = transpose(mine, 0), transpose(other, 1)
        products = [spread(firsts), spread(seconds)]
        sides = mix(place, panels, mine, other, inner, factors)
        updated = None
        for slot in range(0, group, 2):
            pairs = [(v[slot], v[slot + 1]) for v in products + vectors]
            updated = update_step(place, matrix, slot, sides, pairs, updated)
        return updated

    placed = (P("row", "col"), P(None, "row", None), P())
    return jax.shard_map(
        shards, mesh=mesh, in_specs=placed, out_specs=P("row", "col"), check_vma=False
    )
```

```python
import functools

import jax
import jax.numpy as jnp
from jax import lax
from jax.experimental import pallas as pl
from jax.experimental.pallas import tpu as pltpu
from jax.sharding import PartitionSpec as P

F32 = jnp.float32
BF16 = jnp.bfloat16
PLAIN = (((1,), (0,)), ((), ()))
BOTH_LAST = (((1,), (1,)), ((), ()))
BOTH_FIRST = (((0,), (0,)), ((), ()))
VMEM_BYTES = 48 * 1024 * 1024
GATES = (True, True, False, False)
FORWARD = ((0,), (2, 4), (6,))
UPDATE = ((0,), (2, 4), (6,))


def split(values):
    high = values.astype(BF16)
    return high, (values - high.astype(F32)).astype(BF16)


def product(former, latter, dims=PLAIN):
    dot = functools.partial(lax.dot_general, dimension_numbers=dims, preferred_element_type=F32)
    return dot(former[0], latter[0]) + (dot(former[0], latter[1]) + dot(former[1], latter[0]))


def small(former, latter, dims=PLAIN):
    return lax.dot_general(
        former, latter, dims, precision=lax.Precision.HIGHEST, preferred_element_type=F32
    )


def in_order(place, joined, blocks):
    depth, width = blocks[0].shape
    for number, block in enumerate(blocks):
        turn = (place[0] + number) % 2
        rows = pl.ds(pl.multiple_of(turn * depth, depth), depth)
        lanes = slice(number // 2 * width, (number // 2 + 1) * width)
        joined[0][rows, lanes], joined[1][rows, lanes] = split(block[...])


def each_pair(place, joined, blocks, count):
    size = len(blocks) // count
    for turn in range(count):
        now = jnp.logical_and(pl.program_id(0) == turn, pl.program_id(1) == 0)
        pl.when(now)(
            functools.partial(in_order, place, joined, blocks[turn * size : (turn + 1) * size])
        )


def forward_kernel(first, last, count, share, place, block, *refs):
    blocks, refs, joined = refs[: 4 * count], refs[4 * count : -2], refs[-2:]
    pair, step = pl.program_id(0), pl.program_id(1)
    each_pair(place, joined, blocks, count)
    tile = block.shape[0]
    rows = pl.ds(pl.multiple_of(step * tile, tile), tile)
    found = product(split(block[...]), (joined[0][...], joined[1][...]))
    if first:
        own, total, token, high, low, cross = refs
    elif last:
        before, high, low, cross, kept, sent, inner, total = refs
    else:
        before, total, token = refs
    if not last:
        token[...] = jnp.zeros_like(token)

    @pl.when(pair == 0)
    def _():
        total[rows] = found if first else before[rows] + found

    @pl.when(pair != 0)
    def _():
        total[rows] += found

    if first:
        width = own.shape[2]

        @pl.when(pair == 0)
        def _():
            turned = split(jnp.concatenate([own[0, rows].T, own[1, rows].T], axis=0))
            high[step], low[step] = turned
            other = share * product((turned[0][:width], turned[1][:width]), split(own[1, rows]))
            cross[...] = jnp.where(step == 0, 0.0, cross[...]) + other

    if last:
        width = kept.shape[1]

        @pl.when(pair == count - 1)
        def _():
            strip = total[rows]
            one, two = strip[:, :width], strip[:, width:]
            swap = place[1] != 0
            kept[rows] = jnp.where(swap, two, one)
            sent[rows] = jnp.where(swap, one, two)

            @pl.when(step == 0)
            def _():
                inner[...] = jnp.zeros_like(inner)
                inner[3] = cross[...]

            sums = product((high[step], low[step]), split(strip))
            inner[0] += sums[:width, :width]
            inner[1] += sums[width:, :width]
            inner[2] += sums[width:, width:]


def whole(shape):
    return pl.BlockSpec(shape, lambda pair, step, place: (0,) * len(shape))


def forward_step(place, matrix, slots, blocks, own, before, last, share):
    rows = matrix.shape[0]
    depth, width = blocks[0].shape
    tile, count, start = rows // 2, len(slots), slots[0]
    first = before is None
    operands = [matrix, *blocks]
    specs = [
        pl.BlockSpec(
            (tile, 2 * depth),
            lambda pair, step, place: (step, (place[0] ^ (start + 2 * pair)) // 2),
        )
    ]
    total = jax.ShapeDtypeStruct((rows, 2 * width), F32)
    outs, scratch = [total, jax.ShapeDtypeStruct((8, 128), jnp.int32)], []
    if first:
        operands.append(own)
        outs += [jax.ShapeDtypeStruct((2, 2 * width, tile), BF16)] * 2
        outs += [jax.ShapeDtypeStruct((width, width), F32)]
    else:
        operands.append(before[0])
    if last:
        operands += before[2:]
        part = jax.ShapeDtypeStruct((rows, width), F32)
        outs, scratch = [part, part, jax.ShapeDtypeStruct((4, width, width), F32)], [total]
    specs += [whole(operand.shape) for operand in operands[1:]]
    found = pl.pallas_call(
        functools.partial(forward_kernel, first, last, count, share),
        grid_spec=pltpu.PrefetchScalarGridSpec(
            num_scalar_prefetch=1,
            grid=(count, 2),
            in_specs=specs,
            out_specs=[whole(out.shape) for out in outs],
            scratch_shapes=[pltpu.VMEM(one.shape, one.dtype) for one in scratch]
            + [pltpu.VMEM((2 * depth, 2 * width), BF16)] * 2,
        ),
        out_shape=outs,
        compiler_params=pltpu.CompilerParams(vmem_limit_bytes=VMEM_BYTES),
        cost_estimate=pl.CostEstimate(
            flops=6 * rows * depth * 4 * width * count,
            bytes_accessed=8 * rows * depth * count,
            transcendentals=0,
        ),
    )(place, *operands)
    return list(found) if first or last else list(found) + before[2:]


def mix_kernel(place, own, mine, other, inner, factors, high, low):
    one, two = factors[0], factors[1]
    gram_one, cross_yv, gram_old, cross_vv = inner[0], inner[1], inner[2], inner[3]
    correct_one = small(small(one, gram_one, BOTH_FIRST), one)
    cross_wv = small(one, cross_yv, (((0,), (1,)), ((), ()))) - 0.5 * small(
        correct_one, cross_vv, BOTH_FIRST
    )
    drop = small(cross_vv, cross_wv, BOTH_FIRST)
    gram_two = gram_old - drop - small(cross_wv, cross_vv, BOTH_FIRST)
    correct_two = small(small(two, gram_two, BOTH_FIRST), two)
    mixed = -small(small(one, cross_vv), two)
    edge = small(0.5 * small(correct_one, cross_vv) - cross_wv, two)
    swap = place[1] != 0
    y_one = split(jnp.where(swap, other[...], mine[...]))
    y_two = split(jnp.where(swap, mine[...], other[...]))
    v_one, v_two = split(own[0]), split(own[1])
    correct_one = 0.5 * (correct_one + correct_one.T)
    correct_two = 0.5 * (correct_two + correct_two.T)
    one, two, mixed, edge = split(one), split(two), split(mixed), split(edge)
    p_one = product(v_one, one, BOTH_LAST) + product(v_two, mixed, BOTH_LAST)
    p_two = product(v_two, two, BOTH_LAST)
    q_one = product(y_one, one) - product(v_one, split(correct_one)) + product(v_two, edge, BOTH_LAST)
    q_two = product(y_one, mixed) + product(y_two, two) + product(v_one, edge)
    q_two = q_two - product(v_two, split(correct_two))
    turn = place[2] != 0
    parts = (jnp.where(turn, p_two, p_one), jnp.where(turn, p_one, p_two), q_one, q_two)
    width = own.shape[2]
    for number, part in enumerate(parts):
        lanes = slice(number * width, (number + 1) * width)
        high[:, lanes], low[:, lanes] = split(part)


def mix(place, own, *operands):
    _, rows, width = own.shape
    side = jax.ShapeDtypeStruct((rows, 4 * width), BF16)
    vmem = pl.BlockSpec(memory_space=pltpu.VMEM)
    return pl.pallas_call(
        mix_kernel,
        in_specs=[pl.BlockSpec(memory_space=pltpu.SMEM)] + [vmem] * (1 + len(operands)),
        out_specs=[vmem, vmem],
        out_shape=[side, side],
        compiler_params=pltpu.CompilerParams(vmem_limit_bytes=VMEM_BYTES),
        cost_estimate=pl.CostEstimate(
            flops=12 * rows * width * 8 * width, bytes_accessed=32 * rows * width, transcendentals=0
        ),
    )(place, own, *operands)


def update_kernel(count, place, block, high, low, *refs):
    blocks, out, token, joined = refs[: 8 * count], refs[-4], refs[-3], refs[-2:]
    token[...] = jnp.zeros_like(token)
    each_pair(place, joined, blocks, count)
    tile = block.shape[0]
    rows = pl.ds(pl.multiple_of(pl.program_id(1) * tile, tile), tile)
    side = (joined[0][...], joined[1][...])
    out[...] = block[...] - product((high[rows], low[rows]), side, BOTH_LAST)


def update_step(place, matrix, slots, sides, blocks, before):
    rows = matrix.shape[0]
    depth, width = blocks[0].shape
    tile, count, start = rows // 2, len(slots), slots[0]
    block = pl.BlockSpec(
        (tile, 2 * depth),
        lambda pair, step, place: (step, (place[0] ^ (start + 2 * pair)) // 2),
    )
    operands = [matrix, *sides, *blocks]
    specs = [block] + [whole(operand.shape) for operand in operands[1:]]
    aliases = {}
    if before is not None:
        aliases = {1 + len(operands): 0}
        operands.append(before[0])
        specs.append(pl.BlockSpec(memory_space=pl.ANY))
    return pl.pallas_call(
        functools.partial(update_kernel, count),
        grid_spec=pltpu.PrefetchScalarGridSpec(
            num_scalar_prefetch=1,
            grid=(count, 2),
            in_specs=specs,
            out_specs=[block, whole((8, 128))],
            scratch_shapes=[pltpu.VMEM((2 * depth, 4 * width), BF16)] * 2,
        ),
        out_shape=[
            jax.ShapeDtypeStruct(matrix.shape, F32),
            jax.ShapeDtypeStruct((8, 128), jnp.int32),
        ],
        input_output_aliases=aliases,
        compiler_params=pltpu.CompilerParams(vmem_limit_bytes=VMEM_BYTES),
        cost_estimate=pl.CostEstimate(
            flops=6 * rows * depth * 8 * width * count,
            bytes_accessed=16 * rows * depth * count,
            transcendentals=0,
        ),
    )(place, *operands)


def steer(values, cost):
    anywhere = pl.BlockSpec(memory_space=pl.ANY)
    return pl.pallas_call(
        lambda *refs: None,
        in_specs=[anywhere] * len(values),
        out_specs=[anywhere] * len(values),
        out_shape=[jax.ShapeDtypeStruct(part.shape, part.dtype) for part in values],
        input_output_aliases={n: n for n in range(len(values))},
        cost_estimate=pl.CostEstimate(flops=int(cost * 1e9), bytes_accessed=0, transcendentals=0),
    )(*values)


def after(token, values):
    return jnp.where(token[0, 0] != 0, jnp.zeros_like(values), values)


def solution(mesh):
    row_count, col_count = mesh.shape["row"], mesh.shape["col"]
    group = row_count // col_count
    everyone = row_count * col_count
    assert group * col_count == row_count and group >= 4 and everyone & (everyone - 1) == 0
    halves = col_count == 2

    def flip(values, mask):
        return lax.ppermute(values, ("row", "col"), [(n, n ^ mask) for n in range(everyone)])

    def flip_row(values, mask):
        return flip(values, mask * col_count)

    def transpose(values, turn):
        pairs = []
        for s in range(col_count):
            for b in range(group):
                for j in range(col_count):
                    source = (s * group + b) * col_count + j
                    pairs.append((source, ((j - turn) % col_count * group + b) * col_count + s))
        return lax.ppermute(values, ("row", "col"), pairs)

    def spread(own, work, stages, gates):
        found = {0: own}

        def swapped(d, token=None):
            gone = found[d] if token is None else [after(token, part) for part in found[d]]
            return [part for n in range(2) for part in (found[d][n], flip_row(gone[n], 1))]

        if group == 8:
            ahead = flip_row(own[1], 2), flip_row(own[0], 4)
            behind = flip_row(own[0], 2), flip_row(own[1], 4)
            found[2], found[4] = [behind[0], ahead[0]], [ahead[1], behind[1]]
            token = None
            for number, slots in enumerate(stages):
                if 6 in slots:
                    if 6 not in found:
                        found[6] = [flip_row(ahead[1], 2), flip_row(ahead[0], 4)]
                    blocks = [swapped(d, token if gates[1] and d == 6 else None) for d in slots]
                else:
                    blocks = [swapped(d) for d in slots]
                token = work(slots, blocks)
                if number == 0 and gates[0]:
                    gone = [after(token, part) for part in ahead]
                    found[6] = [flip_row(gone[1], 2), flip_row(gone[0], 4)]
            return
        for d in range(2, group, 2):
            found[d] = [flip_row(part, d) for part in own]
        for d in range(0, group, 2):
            work((d,), [swapped(d)])

    def shards(matrix, panels, factors):
        row, col = lax.axis_index("row"), lax.axis_index("col")
        zero = jnp.zeros_like(row)
        place = jnp.stack(
            [row % group, col if halves else zero, row // group if halves else zero]
        ).astype(jnp.int32)
        vectors, sums, outs = {}, [None], [None]

        def forward(slots, blocks):
            vectors.update(zip(slots, blocks))
            sums[0] = forward_step(
                place,
                matrix,
                slots,
                sum(blocks, []),
                panels,
                sums[0],
                slots[-1] + 2 == group,
                1 / col_count,
            )
            return sums[0][1]

        spread([transpose(panels[0], 0), transpose(panels[1], 1)], forward, FORWARD, GATES[:2])
        kept, sent, inner = sums[0]
        if halves:
            mine = kept + flip(sent, 1)
            other = flip(mine, 1)
            blocks = [transpose(mine, 0), transpose(mine, 1)]
        else:
            mine, other = lax.psum((kept, sent), "col")
            blocks = [transpose(mine, 0), transpose(other, 1)]
        blocks = steer(blocks, 40)
        masks = [1 << n for n in range(everyone.bit_length() - 1)]
        for mask in masks[:2]:
            inner = inner + flip(inner, mask)
        masks = masks[2:]
        while masks:
            now, masks = masks[:2], masks[2:]
            reach = now + [now[0] ^ now[1]] if len(now) == 2 else now
            inner = sum([flip(inner, mask) for mask in reach], inner)
        sides = mix(place, panels, mine, other, inner, factors)

        def update(slots, blocks):
            pairs = sum([block + vectors[slot] for slot, block in zip(slots, blocks)], [])
            outs[0] = update_step(place, matrix, slots, sides, pairs, outs[0])
            return outs[0][1]

        spread(blocks, update, UPDATE, GATES[2:])
        return outs[0][0]

    placed = (P("row", "col"), P(None, "row", None), P())
    return jax.shard_map(
        shards, mesh=mesh, in_specs=placed, out_specs=P("row", "col"), check_vma=False
    )
```

```python
import functools

import jax
import jax.numpy as jnp
from jax import lax
from jax.experimental import pallas as pl
from jax.experimental.pallas import tpu as pltpu
from jax.sharding import PartitionSpec as P

F32 = jnp.float32
BF16 = jnp.bfloat16
PLAIN = (((1,), (0,)), ((), ()))
BOTH_LAST = (((1,), (1,)), ((), ()))
BOTH_FIRST = (((0,), (0,)), ((), ()))
VMEM_BYTES = 48 * 1024 * 1024
GATES = (True, True, True, True)
FORWARD = ((0,), (2, 4), (6,))
UPDATE = ((0,), (2, 4), (6,))


def split(values):
    high = values.astype(BF16)
    return high, (values - high.astype(F32)).astype(BF16)


def product(former, latter, dims=PLAIN):
    dot = functools.partial(lax.dot_general, dimension_numbers=dims, preferred_element_type=F32)
    return dot(former[0], latter[0]) + (dot(former[0], latter[1]) + dot(former[1], latter[0]))


def small(former, latter, dims=PLAIN):
    return lax.dot_general(
        former, latter, dims, precision=lax.Precision.HIGHEST, preferred_element_type=F32
    )


def in_order(place, joined, blocks):
    depth, width = blocks[0].shape
    for number, block in enumerate(blocks):
        turn = (place[0] + number) % 2
        rows = pl.ds(pl.multiple_of(turn * depth, depth), depth)
        lanes = slice(number // 2 * width, (number // 2 + 1) * width)
        joined[0][rows, lanes], joined[1][rows, lanes] = split(block[...])


def each_pair(place, joined, blocks, count):
    size = len(blocks) // count
    for turn in range(count):
        now = jnp.logical_and(pl.program_id(0) == turn, pl.program_id(1) == 0)
        pl.when(now)(
            functools.partial(in_order, place, joined, blocks[turn * size : (turn + 1) * size])
        )


def forward_kernel(first, last, count, share, place, block, *refs):
    blocks, refs, joined = refs[: 4 * count], refs[4 * count : -2], refs[-2:]
    pair, step = pl.program_id(0), pl.program_id(1)
    each_pair(place, joined, blocks, count)
    tile = block.shape[0]
    rows = pl.ds(pl.multiple_of(step * tile, tile), tile)
    found = product(split(block[...]), (joined[0][...], joined[1][...]))
    if first:
        own, total, token, high, low, cross = refs
    elif last:
        before, high, low, cross, kept, sent, inner, total = refs
    else:
        before, total, token = refs
    if not last:
        token[...] = jnp.zeros_like(token)

    @pl.when(pair == 0)
    def _():
        total[rows] = found if first else before[rows] + found

    @pl.when(pair != 0)
    def _():
        total[rows] += found

    if first:
        width = own.shape[2]

        @pl.when(pair == 0)
        def _():
            turned = split(jnp.concatenate([own[0, rows].T, own[1, rows].T], axis=0))
            high[step], low[step] = turned
            other = share * product((turned[0][:width], turned[1][:width]), split(own[1, rows]))
            cross[...] = jnp.where(step == 0, 0.0, cross[...]) + other

    if last:
        width = kept.shape[1]

        @pl.when(pair == count - 1)
        def _():
            strip = total[rows]
            one, two = strip[:, :width], strip[:, width:]
            swap = place[1] != 0
            kept[rows] = jnp.where(swap, two, one)
            sent[rows] = jnp.where(swap, one, two)

            @pl.when(step == 0)
            def _():
                inner[...] = jnp.zeros_like(inner)
                inner[3] = cross[...]

            sums = product((high[step], low[step]), split(strip))
            inner[0] += sums[:width, :width]
            inner[1] += sums[width:, :width]
            inner[2] += sums[width:, width:]


def whole(shape):
    return pl.BlockSpec(shape, lambda pair, step, place: (0,) * len(shape))


def forward_step(place, matrix, slots, blocks, own, before, last, share):
    rows = matrix.shape[0]
    depth, width = blocks[0].shape
    tile, count, start = rows // 2, len(slots), slots[0]
    first = before is None
    operands = [matrix, *blocks]
    specs = [
        pl.BlockSpec(
            (tile, 2 * depth),
            lambda pair, step, place: (step, (place[0] ^ (start + 2 * pair)) // 2),
        )
    ]
    total = jax.ShapeDtypeStruct((rows, 2 * width), F32)
    outs, scratch = [total, jax.ShapeDtypeStruct((8, 128), jnp.int32)], []
    if first:
        operands.append(own)
        outs += [jax.ShapeDtypeStruct((2, 2 * width, tile), BF16)] * 2
        outs += [jax.ShapeDtypeStruct((width, width), F32)]
    else:
        operands.append(before[0])
    if last:
        operands += before[2:]
        part = jax.ShapeDtypeStruct((rows, width), F32)
        outs, scratch = [part, part, jax.ShapeDtypeStruct((4, width, width), F32)], [total]
    specs += [whole(operand.shape) for operand in operands[1:]]
    found = pl.pallas_call(
        functools.partial(forward_kernel, first, last, count, share),
        grid_spec=pltpu.PrefetchScalarGridSpec(
            num_scalar_prefetch=1,
            grid=(count, 2),
            in_specs=specs,
            out_specs=[whole(out.shape) for out in outs],
            scratch_shapes=[pltpu.VMEM(one.shape, one.dtype) for one in scratch]
            + [pltpu.VMEM((2 * depth, 2 * width), BF16)] * 2,
        ),
        out_shape=outs,
        compiler_params=pltpu.CompilerParams(vmem_limit_bytes=VMEM_BYTES),
        cost_estimate=pl.CostEstimate(
            flops=6 * rows * depth * 4 * width * count,
            bytes_accessed=8 * rows * depth * count,
            transcendentals=0,
        ),
    )(place, *operands)
    return list(found) if first or last else list(found) + before[2:]


def mix_kernel(place, own, mine, other, inner, factors, high, low):
    one, two = factors[0], factors[1]
    gram_one, cross_yv, gram_old, cross_vv = inner[0], inner[1], inner[2], inner[3]
    correct_one = small(small(one, gram_one, BOTH_FIRST), one)
    cross_wv = small(one, cross_yv, (((0,), (1,)), ((), ()))) - 0.5 * small(
        correct_one, cross_vv, BOTH_FIRST
    )
    drop = small(cross_vv, cross_wv, BOTH_FIRST)
    gram_two = gram_old - drop - small(cross_wv, cross_vv, BOTH_FIRST)
    correct_two = small(small(two, gram_two, BOTH_FIRST), two)
    mixed = -small(small(one, cross_vv), two)
    edge = small(0.5 * small(correct_one, cross_vv) - cross_wv, two)
    swap = place[1] != 0
    y_one = split(jnp.where(swap, other[...], mine[...]))
    y_two = split(jnp.where(swap, mine[...], other[...]))
    v_one, v_two = split(own[0]), split(own[1])
    correct_one = 0.5 * (correct_one + correct_one.T)
    correct_two = 0.5 * (correct_two + correct_two.T)
    one, two, mixed, edge = split(one), split(two), split(mixed), split(edge)
    p_one = product(v_one, one, BOTH_LAST) + product(v_two, mixed, BOTH_LAST)
    p_two = product(v_two, two, BOTH_LAST)
    q_one = product(y_one, one) - product(v_one, split(correct_one)) + product(v_two, edge, BOTH_LAST)
    q_two = product(y_one, mixed) + product(y_two, two) + product(v_one, edge)
    q_two = q_two - product(v_two, split(correct_two))
    turn = place[2] != 0
    parts = (jnp.where(turn, p_two, p_one), jnp.where(turn, p_one, p_two), q_one, q_two)
    width = own.shape[2]
    for number, part in enumerate(parts):
        lanes = slice(number * width, (number + 1) * width)
        high[:, lanes], low[:, lanes] = split(part)


def mix(place, own, *operands):
    _, rows, width = own.shape
    side = jax.ShapeDtypeStruct((rows, 4 * width), BF16)
    vmem = pl.BlockSpec(memory_space=pltpu.VMEM)
    return pl.pallas_call(
        mix_kernel,
        in_specs=[pl.BlockSpec(memory_space=pltpu.SMEM)] + [vmem] * (1 + len(operands)),
        out_specs=[vmem, vmem],
        out_shape=[side, side],
        compiler_params=pltpu.CompilerParams(vmem_limit_bytes=VMEM_BYTES),
        cost_estimate=pl.CostEstimate(
            flops=12 * rows * width * 8 * width, bytes_accessed=32 * rows * width, transcendentals=0
        ),
    )(place, own, *operands)


def update_kernel(count, place, block, high, low, *refs):
    blocks, out, token, joined = refs[: 8 * count], refs[-4], refs[-3], refs[-2:]
    token[...] = jnp.zeros_like(token)
    each_pair(place, joined, blocks, count)
    tile = block.shape[0]
    rows = pl.ds(pl.multiple_of(pl.program_id(1) * tile, tile), tile)
    side = (joined[0][...], joined[1][...])
    out[...] = block[...] - product((high[rows], low[rows]), side, BOTH_LAST)


def update_step(place, matrix, slots, sides, blocks, before):
    rows = matrix.shape[0]
    depth, width = blocks[0].shape
    tile, count, start = rows // 2, len(slots), slots[0]
    block = pl.BlockSpec(
        (tile, 2 * depth),
        lambda pair, step, place: (step, (place[0] ^ (start + 2 * pair)) // 2),
    )
    operands = [matrix, *sides, *blocks]
    specs = [block] + [whole(operand.shape) for operand in operands[1:]]
    aliases = {}
    if before is not None:
        aliases = {1 + len(operands): 0}
        operands.append(before[0])
        specs.append(pl.BlockSpec(memory_space=pl.ANY))
    return pl.pallas_call(
        functools.partial(update_kernel, count),
        grid_spec=pltpu.PrefetchScalarGridSpec(
            num_scalar_prefetch=1,
            grid=(count, 2),
            in_specs=specs,
            out_specs=[block, whole((8, 128))],
            scratch_shapes=[pltpu.VMEM((2 * depth, 4 * width), BF16)] * 2,
        ),
        out_shape=[
            jax.ShapeDtypeStruct(matrix.shape, F32),
            jax.ShapeDtypeStruct((8, 128), jnp.int32),
        ],
        input_output_aliases=aliases,
        compiler_params=pltpu.CompilerParams(vmem_limit_bytes=VMEM_BYTES),
        cost_estimate=pl.CostEstimate(
            flops=6 * rows * depth * 8 * width * count,
            bytes_accessed=16 * rows * depth * count,
            transcendentals=0,
        ),
    )(place, *operands)


def steer(values, cost):
    anywhere = pl.BlockSpec(memory_space=pl.ANY)
    return pl.pallas_call(
        lambda *refs: None,
        in_specs=[anywhere] * len(values),
        out_specs=[anywhere] * len(values),
        out_shape=[jax.ShapeDtypeStruct(part.shape, part.dtype) for part in values],
        input_output_aliases={n: n for n in range(len(values))},
        cost_estimate=pl.CostEstimate(flops=int(cost * 1e9), bytes_accessed=0, transcendentals=0),
    )(*values)


def after(token, values):
    return jnp.where(token[0, 0] != 0, jnp.zeros_like(values), values)


def solution(mesh):
    row_count, col_count = mesh.shape["row"], mesh.shape["col"]
    group = row_count // col_count
    everyone = row_count * col_count
    assert group * col_count == row_count and group >= 4 and everyone & (everyone - 1) == 0
    halves = col_count == 2

    def flip(values, mask):
        return lax.ppermute(values, ("row", "col"), [(n, n ^ mask) for n in range(everyone)])

    def flip_row(values, mask):
        return flip(values, mask * col_count)

    def transpose(values, turn):
        pairs = []
        for s in range(col_count):
            for b in range(group):
                for j in range(col_count):
                    source = (s * group + b) * col_count + j
                    pairs.append((source, ((j - turn) % col_count * group + b) * col_count + s))
        return lax.ppermute(values, ("row", "col"), pairs)

    def spread(own, work, stages, gates):
        found = {0: own}

        def swapped(d, token=None):
            gone = found[d] if token is None else [after(token, part) for part in found[d]]
            return [part for n in range(2) for part in (found[d][n], flip_row(gone[n], 1))]

        if group == 8:
            ahead = flip_row(own[1], 2), flip_row(own[0], 4)
            behind = flip_row(own[0], 2), flip_row(own[1], 4)
            found[2], found[4] = [behind[0], ahead[0]], [ahead[1], behind[1]]
            token = None
            for number, slots in enumerate(stages):
                if 6 in slots:
                    if 6 not in found:
                        found[6] = [flip_row(ahead[1], 2), flip_row(ahead[0], 4)]
                    blocks = [swapped(d, token if gates[1] and d == 6 else None) for d in slots]
                else:
                    blocks = [swapped(d) for d in slots]
                token = work(slots, blocks)
                if number == 0 and gates[0]:
                    gone = [after(token, part) for part in ahead]
                    found[6] = [flip_row(gone[1], 2), flip_row(gone[0], 4)]
            return
        for d in range(2, group, 2):
            found[d] = [flip_row(part, d) for part in own]
        for d in range(0, group, 2):
            work((d,), [swapped(d)])

    def shards(matrix, panels, factors):
        row, col = lax.axis_index("row"), lax.axis_index("col")
        zero = jnp.zeros_like(row)
        place = jnp.stack(
            [row % group, col if halves else zero, row // group if halves else zero]
        ).astype(jnp.int32)
        vectors, sums, outs = {}, [None], [None]

        def forward(slots, blocks):
            vectors.update(zip(slots, blocks))
            sums[0] = forward_step(
                place,
                matrix,
                slots,
                sum(blocks, []),
                panels,
                sums[0],
                slots[-1] + 2 == group,
                1 / col_count,
            )
            return sums[0][1]

        spread([transpose(panels[0], 0), transpose(panels[1], 1)], forward, FORWARD, GATES[:2])
        kept, sent, inner = sums[0]
        if halves:
            mine = kept + flip(sent, 1)
            other = flip(mine, 1)
            blocks = [transpose(mine, 0), transpose(mine, 1)]
        else:
            mine, other = lax.psum((kept, sent), "col")
            blocks = [transpose(mine, 0), transpose(other, 1)]
        blocks = steer(blocks, 40)
        odd = row % 2 != 0
        upper, lower = inner[:2], inner[2:]
        part = jnp.where(odd, lower, upper) + flip_row(jnp.where(odd, upper, lower), 1)
        masks = [1 << n for n in range(everyone.bit_length() - 1) if 1 << n != col_count]
        for mask in masks:
            part = part + flip(part, mask)
        there = flip_row(part, 1)
        inner = jnp.concatenate([jnp.where(odd, there, part), jnp.where(odd, part, there)], axis=0)
        sides = mix(place, panels, mine, other, inner, factors)

        def update(slots, blocks):
            pairs = sum([block + vectors[slot] for slot, block in zip(slots, blocks)], [])
            outs[0] = update_step(place, matrix, slots, sides, pairs, outs[0])
            return outs[0][1]

        spread(blocks, update, UPDATE, GATES[2:])
        return outs[0][0]

    placed = (P("row", "col"), P(None, "row", None), P())
    return jax.shard_map(
        shards, mesh=mesh, in_specs=placed, out_specs=P("row", "col"), check_vma=False
    )
```

```python
import functools

import jax
import jax.numpy as jnp
from jax import lax
from jax.experimental import pallas as pl
from jax.experimental.pallas import tpu as pltpu
from jax.sharding import PartitionSpec as P

F32 = jnp.float32
BF16 = jnp.bfloat16
PLAIN = (((1,), (0,)), ((), ()))
BOTH_LAST = (((1,), (1,)), ((), ()))
BOTH_FIRST = (((0,), (0,)), ((), ()))
VMEM_BYTES = 36 * 1024 * 1024
GATES = (True, True, True, True)
FORWARD = ((0,), (2, 4), (6,))
UPDATE = ((0,), (2, 4), (6,))


def split(values):
    high = values.astype(BF16)
    return high, (values - high.astype(F32)).astype(BF16)


def product(former, latter, dims=PLAIN):
    dot = functools.partial(lax.dot_general, dimension_numbers=dims, preferred_element_type=F32)
    return dot(former[0], latter[0]) + (dot(former[0], latter[1]) + dot(former[1], latter[0]))


def small(former, latter, dims=PLAIN):
    return lax.dot_general(
        former, latter, dims, precision=lax.Precision.HIGHEST, preferred_element_type=F32
    )


def in_order(place, joined, blocks):
    depth, width = blocks[0].shape
    for number, block in enumerate(blocks):
        turn = (place[0] + number) % 2
        rows = pl.ds(pl.multiple_of(turn * depth, depth), depth)
        lanes = slice(number // 2 * width, (number // 2 + 1) * width)
        joined[0][rows, lanes], joined[1][rows, lanes] = split(block[...])


def each_pair(place, joined, blocks, count):
    size = len(blocks) // count
    for turn in range(count):
        now = jnp.logical_and(pl.program_id(0) == turn, pl.program_id(1) == 0)
        pl.when(now)(
            functools.partial(in_order, place, joined, blocks[turn * size : (turn + 1) * size])
        )


def forward_kernel(first, last, count, share, place, block, *refs):
    blocks, refs, joined = refs[: 4 * count], refs[4 * count : -2], refs[-2:]
    pair, step = pl.program_id(0), pl.program_id(1)
    each_pair(place, joined, blocks, count)
    tile = block.shape[0]
    rows = pl.ds(pl.multiple_of(step * tile, tile), tile)
    found = product(split(block[...]), (joined[0][...], joined[1][...]))
    if first:
        own, total, token, high, low, cross = refs
    elif last:
        before, high, low, cross, kept, sent, inner, total = refs
    else:
        before, total, token = refs
    if not last:
        token[...] = jnp.zeros_like(token)

    @pl.when(pair == 0)
    def _():
        total[rows] = found if first else before[rows] + found

    @pl.when(pair != 0)
    def _():
        total[rows] += found

    if first:
        width = own.shape[2]

        @pl.when(pair == 0)
        def _():
            turned = split(jnp.concatenate([own[0, rows].T, own[1, rows].T], axis=0))
            high[step], low[step] = turned
            other = share * product((turned[0][:width], turned[1][:width]), split(own[1, rows]))
            cross[...] = jnp.where(step == 0, 0.0, cross[...]) + other

    if last:
        width = kept.shape[1]

        @pl.when(pair == count - 1)
        def _():
            strip = total[rows]
            one, two = strip[:, :width], strip[:, width:]
            swap = place[1] != 0
            kept[rows] = jnp.where(swap, two, one)
            sent[rows] = jnp.where(swap, one, two)

            @pl.when(step == 0)
            def _():
                inner[...] = jnp.zeros_like(inner)
                inner[3] = cross[...]

            sums = product((high[step], low[step]), split(strip))
            inner[0] += sums[:width, :width]
            inner[1] += sums[width:, :width]
            inner[2] += sums[width:, width:]


def whole(shape):
    return pl.BlockSpec(shape, lambda pair, step, place: (0,) * len(shape))


def forward_step(place, matrix, slots, blocks, own, before, last, share):
    rows = matrix.shape[0]
    depth, width = blocks[0].shape
    tile, count, start = rows // 2, len(slots), slots[0]
    first = before is None
    operands = [matrix, *blocks]
    specs = [
        pl.BlockSpec(
            (tile, 2 * depth),
            lambda pair, step, place: (step, (place[0] ^ (start + 2 * pair)) // 2),
        )
    ]
    total = jax.ShapeDtypeStruct((rows, 2 * width), F32)
    outs, scratch = [total, jax.ShapeDtypeStruct((8, 128), jnp.int32)], []
    if first:
        operands.append(own)
        outs += [jax.ShapeDtypeStruct((2, 2 * width, tile), BF16)] * 2
        outs += [jax.ShapeDtypeStruct((width, width), F32)]
    else:
        operands.append(before[0])
    if last:
        operands += before[2:]
        part = jax.ShapeDtypeStruct((rows, width), F32)
        outs, scratch = [part, part, jax.ShapeDtypeStruct((4, width, width), F32)], [total]
    specs += [whole(operand.shape) for operand in operands[1:]]
    found = pl.pallas_call(
        functools.partial(forward_kernel, first, last, count, share),
        grid_spec=pltpu.PrefetchScalarGridSpec(
            num_scalar_prefetch=1,
            grid=(count, 2),
            in_specs=specs,
            out_specs=[whole(out.shape) for out in outs],
            scratch_shapes=[pltpu.VMEM(one.shape, one.dtype) for one in scratch]
            + [pltpu.VMEM((2 * depth, 2 * width), BF16)] * 2,
        ),
        out_shape=outs,
        compiler_params=pltpu.CompilerParams(vmem_limit_bytes=VMEM_BYTES),
        cost_estimate=pl.CostEstimate(
            flops=6 * rows * depth * 4 * width * count,
            bytes_accessed=8 * rows * depth * count,
            transcendentals=0,
        ),
    )(place, *operands)
    return list(found) if first or last else list(found) + before[2:]


def mix_kernel(place, own, mine, other, inner, factors, high, low):
    one, two = factors[0], factors[1]
    gram_one, cross_yv, gram_old, cross_vv = inner[0], inner[1], inner[2], inner[3]
    correct_one = small(small(one, gram_one, BOTH_FIRST), one)
    cross_wv = small(one, cross_yv, (((0,), (1,)), ((), ()))) - 0.5 * small(
        correct_one, cross_vv, BOTH_FIRST
    )
    drop = small(cross_vv, cross_wv, BOTH_FIRST)
    gram_two = gram_old - drop - small(cross_wv, cross_vv, BOTH_FIRST)
    correct_two = small(small(two, gram_two, BOTH_FIRST), two)
    mixed = -small(small(one, cross_vv), two)
    edge = small(0.5 * small(correct_one, cross_vv) - cross_wv, two)
    swap = place[1] != 0
    y_one = split(jnp.where(swap, other[...], mine[...]))
    y_two = split(jnp.where(swap, mine[...], other[...]))
    v_one, v_two = split(own[0]), split(own[1])
    correct_one = 0.5 * (correct_one + correct_one.T)
    correct_two = 0.5 * (correct_two + correct_two.T)
    one, two, mixed, edge = split(one), split(two), split(mixed), split(edge)
    p_one = product(v_one, one, BOTH_LAST) + product(v_two, mixed, BOTH_LAST)
    p_two = product(v_two, two, BOTH_LAST)
    q_one = product(y_one, one) - product(v_one, split(correct_one)) + product(v_two, edge, BOTH_LAST)
    q_two = product(y_one, mixed) + product(y_two, two) + product(v_one, edge)
    q_two = q_two - product(v_two, split(correct_two))
    turn = place[2] != 0
    parts = (jnp.where(turn, p_two, p_one), jnp.where(turn, p_one, p_two), q_one, q_two)
    width = own.shape[2]
    for number, part in enumerate(parts):
        lanes = slice(number * width, (number + 1) * width)
        high[:, lanes], low[:, lanes] = split(part)


def mix(place, own, *operands):
    _, rows, width = own.shape
    side = jax.ShapeDtypeStruct((rows, 4 * width), BF16)
    vmem = pl.BlockSpec(memory_space=pltpu.VMEM)
    return pl.pallas_call(
        mix_kernel,
        in_specs=[pl.BlockSpec(memory_space=pltpu.SMEM)] + [vmem] * (1 + len(operands)),
        out_specs=[vmem, vmem],
        out_shape=[side, side],
        compiler_params=pltpu.CompilerParams(vmem_limit_bytes=VMEM_BYTES),
        cost_estimate=pl.CostEstimate(
            flops=12 * rows * width * 8 * width, bytes_accessed=32 * rows * width, transcendentals=0
        ),
    )(place, own, *operands)


def update_kernel(count, place, block, high, low, *refs):
    blocks, out, token, joined = refs[: 8 * count], refs[-4], refs[-3], refs[-2:]
    token[...] = jnp.zeros_like(token)
    each_pair(place, joined, blocks, count)
    tile = block.shape[0]
    rows = pl.ds(pl.multiple_of(pl.program_id(1) * tile, tile), tile)
    side = (joined[0][...], joined[1][...])
    out[...] = block[...] - product((high[rows], low[rows]), side, BOTH_LAST)


def update_step(place, matrix, slots, sides, blocks, before):
    rows = matrix.shape[0]
    depth, width = blocks[0].shape
    tile, count, start = rows // 2, len(slots), slots[0]
    block = pl.BlockSpec(
        (tile, 2 * depth),
        lambda pair, step, place: (step, (place[0] ^ (start + 2 * pair)) // 2),
    )
    operands = [matrix, *sides, *blocks]
    specs = [block] + [whole(operand.shape) for operand in operands[1:]]
    aliases = {}
    if before is not None:
        aliases = {1 + len(operands): 0}
        operands.append(before[0])
        specs.append(pl.BlockSpec(memory_space=pl.ANY))
    return pl.pallas_call(
        functools.partial(update_kernel, count),
        grid_spec=pltpu.PrefetchScalarGridSpec(
            num_scalar_prefetch=1,
            grid=(count, 2),
            in_specs=specs,
            out_specs=[block, whole((8, 128))],
            scratch_shapes=[pltpu.VMEM((2 * depth, 4 * width), BF16)] * 2,
        ),
        out_shape=[
            jax.ShapeDtypeStruct(matrix.shape, F32),
            jax.ShapeDtypeStruct((8, 128), jnp.int32),
        ],
        input_output_aliases=aliases,
        compiler_params=pltpu.CompilerParams(vmem_limit_bytes=VMEM_BYTES),
        cost_estimate=pl.CostEstimate(
            flops=6 * rows * depth * 8 * width * count,
            bytes_accessed=16 * rows * depth * count,
            transcendentals=0,
        ),
    )(place, *operands)


def steer(values, cost):
    anywhere = pl.BlockSpec(memory_space=pl.ANY)
    return pl.pallas_call(
        lambda *refs: None,
        in_specs=[anywhere] * len(values),
        out_specs=[anywhere] * len(values),
        out_shape=[jax.ShapeDtypeStruct(part.shape, part.dtype) for part in values],
        input_output_aliases={n: n for n in range(len(values))},
        cost_estimate=pl.CostEstimate(flops=int(cost * 1e9), bytes_accessed=0, transcendentals=0),
    )(*values)


def after(token, values):
    return jnp.where(token[0, 0] != 0, jnp.zeros_like(values), values)


def solution(mesh):
    row_count, col_count = mesh.shape["row"], mesh.shape["col"]
    group = row_count // col_count
    everyone = row_count * col_count
    assert group * col_count == row_count and group >= 4 and everyone & (everyone - 1) == 0
    halves = col_count == 2

    def flip(values, mask):
        return lax.ppermute(values, ("row", "col"), [(n, n ^ mask) for n in range(everyone)])

    def flip_row(values, mask):
        return flip(values, mask * col_count)

    def transpose(values, turn):
        pairs = []
        for s in range(col_count):
            for b in range(group):
                for j in range(col_count):
                    source = (s * group + b) * col_count + j
                    pairs.append((source, ((j - turn) % col_count * group + b) * col_count + s))
        return lax.ppermute(values, ("row", "col"), pairs)

    def spread(own, work, stages, gates):
        found = {0: own}

        def swapped(d, token=None):
            gone = found[d] if token is None else [after(token, part) for part in found[d]]
            return [part for n in range(2) for part in (found[d][n], flip_row(gone[n], 1))]

        if group == 8:
            ahead = flip_row(own[1], 2), flip_row(own[0], 4)
            behind = flip_row(own[0], 2), flip_row(own[1], 4)
            found[2], found[4] = [behind[0], ahead[0]], [ahead[1], behind[1]]
            token = None
            for number, slots in enumerate(stages):
                if 6 in slots:
                    if 6 not in found:
                        found[6] = [flip_row(ahead[1], 2), flip_row(ahead[0], 4)]
                    blocks = [swapped(d, token if gates[1] and d == 6 else None) for d in slots]
                else:
                    blocks = [swapped(d) for d in slots]
                token = work(slots, blocks)
                if number == 0 and gates[0]:
                    gone = [after(token, part) for part in ahead]
                    found[6] = [flip_row(gone[1], 2), flip_row(gone[0], 4)]
            return
        for d in range(2, group, 2):
            found[d] = [flip_row(part, d) for part in own]
        for d in range(0, group, 2):
            work((d,), [swapped(d)])

    def shards(matrix, panels, factors):
        row, col = lax.axis_index("row"), lax.axis_index("col")
        zero = jnp.zeros_like(row)
        place = jnp.stack(
            [row % group, col if halves else zero, row // group if halves else zero]
        ).astype(jnp.int32)
        vectors, sums, outs = {}, [None], [None]

        def forward(slots, blocks):
            vectors.update(zip(slots, blocks))
            sums[0] = forward_step(
                place,
                matrix,
                slots,
                sum(blocks, []),
                panels,
                sums[0],
                slots[-1] + 2 == group,
                1 / col_count,
            )
            return sums[0][1]

        spread([transpose(panels[0], 0), transpose(panels[1], 1)], forward, FORWARD, GATES[:2])
        kept, sent, inner = sums[0]
        if halves:
            mine = kept + flip(sent, 1)
            other = flip(mine, 1)
            blocks = [transpose(mine, 0), transpose(mine, 1)]
        else:
            mine, other = lax.psum((kept, sent), "col")
            blocks = [transpose(mine, 0), transpose(other, 1)]
        blocks = steer(blocks, 40)
        odd = row % 2 != 0
        upper, lower = inner[:2], inner[2:]
        part = jnp.where(odd, lower, upper) + flip_row(jnp.where(odd, upper, lower), 1)
        masks = [1 << n for n in range(everyone.bit_length() - 1) if 1 << n != col_count]
        for mask in masks:
            part = part + flip(part, mask)
        there = flip_row(part, 1)
        inner = jnp.concatenate([jnp.where(odd, there, part), jnp.where(odd, part, there)], axis=0)
        sides = mix(place, panels, mine, other, inner, factors)

        def update(slots, blocks):
            pairs = sum([block + vectors[slot] for slot, block in zip(slots, blocks)], [])
            outs[0] = update_step(place, matrix, slots, sides, pairs, outs[0])
            return outs[0][1]

        spread(blocks, update, UPDATE, GATES[2:])
        return outs[0][0]

    placed = (P("row", "col"), P(None, "row", None), P())
    return jax.shard_map(
        shards, mesh=mesh, in_specs=placed, out_specs=P("row", "col"), check_vma=False
    )
```

```python
import functools

import jax
import jax.numpy as jnp
from jax import lax
from jax.experimental import pallas as pl
from jax.experimental.pallas import tpu as pltpu
from jax.sharding import PartitionSpec as P

F32 = jnp.float32
BF16 = jnp.bfloat16
PLAIN = (((1,), (0,)), ((), ()))
BOTH_LAST = (((1,), (1,)), ((), ()))
BOTH_FIRST = (((0,), (0,)), ((), ()))
VMEM_BYTES = 36 * 1024 * 1024
GATES = (True, True, True, True)
FORWARD = ((0,), (2, 4), (6,))
UPDATE = ((0,), (2, 4), (6,))


def split(values):
    high = values.astype(BF16)
    return high, (values - high.astype(F32)).astype(BF16)


def product(former, latter, dims=PLAIN):
    dot = functools.partial(lax.dot_general, dimension_numbers=dims, preferred_element_type=F32)
    return dot(former[0], latter[0]) + (dot(former[0], latter[1]) + dot(former[1], latter[0]))


def small(former, latter, dims=PLAIN):
    return product(split(former), split(latter), dims)


def in_order(place, joined, blocks):
    depth, width = blocks[0].shape
    for number, block in enumerate(blocks):
        turn = (place[0] + number) % 2
        rows = pl.ds(pl.multiple_of(turn * depth, depth), depth)
        lanes = slice(number // 2 * width, (number // 2 + 1) * width)
        joined[0][rows, lanes], joined[1][rows, lanes] = split(block[...])


def each_pair(place, joined, blocks, count):
    size = len(blocks) // count
    for turn in range(count):
        now = jnp.logical_and(pl.program_id(0) == turn, pl.program_id(1) == 0)
        pl.when(now)(
            functools.partial(in_order, place, joined, blocks[turn * size : (turn + 1) * size])
        )


def forward_kernel(first, last, count, share, place, block, *refs):
    blocks, refs, joined = refs[: 4 * count], refs[4 * count : -2], refs[-2:]
    pair, step = pl.program_id(0), pl.program_id(1)
    each_pair(place, joined, blocks, count)
    tile = block.shape[0]
    rows = pl.ds(pl.multiple_of(step * tile, tile), tile)
    found = product(split(block[...]), (joined[0][...], joined[1][...]))
    if first:
        own, total, token, high, low, cross = refs
    elif last:
        before, high, low, cross, kept, sent, inner, total = refs
    else:
        before, total, token = refs
    if not last:
        token[...] = jnp.zeros_like(token)

    @pl.when(pair == 0)
    def _():
        total[rows] = found if first else before[rows] + found

    @pl.when(pair != 0)
    def _():
        total[rows] += found

    if first:
        width = own.shape[2]

        @pl.when(pair == 0)
        def _():
            turned = split(jnp.concatenate([own[0, rows].T, own[1, rows].T], axis=0))
            high[step], low[step] = turned
            other = share * product((turned[0][:width], turned[1][:width]), split(own[1, rows]))
            cross[...] = jnp.where(step == 0, 0.0, cross[...]) + other

    if last:
        width = kept.shape[1]

        @pl.when(pair == count - 1)
        def _():
            strip = total[rows]
            one, two = strip[:, :width], strip[:, width:]
            swap = place[1] != 0
            kept[rows] = jnp.where(swap, two, one)
            sent[rows] = jnp.where(swap, one, two)

            @pl.when(step == 0)
            def _():
                inner[...] = jnp.zeros_like(inner)
                inner[3] = cross[...]

            sums = product((high[step], low[step]), split(strip))
            inner[0] += sums[:width, :width]
            inner[1] += sums[width:, :width]
            inner[2] += sums[width:, width:]


def whole(shape):
    return pl.BlockSpec(shape, lambda pair, step, place: (0,) * len(shape))


def forward_step(place, matrix, slots, blocks, own, before, last, share):
    rows = matrix.shape[0]
    depth, width = blocks[0].shape
    tile, count, start = rows // 2, len(slots), slots[0]
    first = before is None
    operands = [matrix, *blocks]
    specs = [
        pl.BlockSpec(
            (tile, 2 * depth),
            lambda pair, step, place: (step, (place[0] ^ (start + 2 * pair)) // 2),
        )
    ]
    total = jax.ShapeDtypeStruct((rows, 2 * width), F32)
    outs, scratch = [total, jax.ShapeDtypeStruct((8, 128), jnp.int32)], []
    if first:
        operands.append(own)
        outs += [jax.ShapeDtypeStruct((2, 2 * width, tile), BF16)] * 2
        outs += [jax.ShapeDtypeStruct((width, width), F32)]
    else:
        operands.append(before[0])
    if last:
        operands += before[2:]
        part = jax.ShapeDtypeStruct((rows, width), F32)
        outs, scratch = [part, part, jax.ShapeDtypeStruct((4, width, width), F32)], [total]
    specs += [whole(operand.shape) for operand in operands[1:]]
    found = pl.pallas_call(
        functools.partial(forward_kernel, first, last, count, share),
        grid_spec=pltpu.PrefetchScalarGridSpec(
            num_scalar_prefetch=1,
            grid=(count, 2),
            in_specs=specs,
            out_specs=[whole(out.shape) for out in outs],
            scratch_shapes=[pltpu.VMEM(one.shape, one.dtype) for one in scratch]
            + [pltpu.VMEM((2 * depth, 2 * width), BF16)] * 2,
        ),
        out_shape=outs,
        compiler_params=pltpu.CompilerParams(vmem_limit_bytes=VMEM_BYTES),
        cost_estimate=pl.CostEstimate(
            flops=6 * rows * depth * 4 * width * count,
            bytes_accessed=8 * rows * depth * count,
            transcendentals=0,
        ),
    )(place, *operands)
    return list(found) if first or last else list(found) + before[2:]


def mix_kernel(place, own, mine, other, inner, factors, high, low):
    one, two = factors[0], factors[1]
    gram_one, cross_yv, gram_old, cross_vv = inner[0], inner[1], inner[2], inner[3]
    correct_one = small(small(one, gram_one, BOTH_FIRST), one)
    cross_wv = small(one, cross_yv, (((0,), (1,)), ((), ()))) - 0.5 * small(
        correct_one, cross_vv, BOTH_FIRST
    )
    drop = small(cross_vv, cross_wv, BOTH_FIRST)
    gram_two = gram_old - drop - small(cross_wv, cross_vv, BOTH_FIRST)
    correct_two = small(small(two, gram_two, BOTH_FIRST), two)
    mixed = -small(small(one, cross_vv), two)
    edge = small(0.5 * small(correct_one, cross_vv) - cross_wv, two)
    swap = place[1] != 0
    y_one = split(jnp.where(swap, other[...], mine[...]))
    y_two = split(jnp.where(swap, mine[...], other[...]))
    v_one, v_two = split(own[0]), split(own[1])
    correct_one = 0.5 * (correct_one + correct_one.T)
    correct_two = 0.5 * (correct_two + correct_two.T)
    one, two, mixed, edge = split(one), split(two), split(mixed), split(edge)
    p_one = product(v_one, one, BOTH_LAST) + product(v_two, mixed, BOTH_LAST)
    p_two = product(v_two, two, BOTH_LAST)
    q_one = product(y_one, one) - product(v_one, split(correct_one)) + product(v_two, edge, BOTH_LAST)
    q_two = product(y_one, mixed) + product(y_two, two) + product(v_one, edge)
    q_two = q_two - product(v_two, split(correct_two))
    turn = place[2] != 0
    parts = (jnp.where(turn, p_two, p_one), jnp.where(turn, p_one, p_two), q_one, q_two)
    width = own.shape[2]
    for number, part in enumerate(parts):
        lanes = slice(number * width, (number + 1) * width)
        high[:, lanes], low[:, lanes] = split(part)


def mix(place, own, *operands):
    _, rows, width = own.shape
    side = jax.ShapeDtypeStruct((rows, 4 * width), BF16)
    vmem = pl.BlockSpec(memory_space=pltpu.VMEM)
    return pl.pallas_call(
        mix_kernel,
        in_specs=[pl.BlockSpec(memory_space=pltpu.SMEM)] + [vmem] * (1 + len(operands)),
        out_specs=[vmem, vmem],
        out_shape=[side, side],
        compiler_params=pltpu.CompilerParams(vmem_limit_bytes=VMEM_BYTES),
        cost_estimate=pl.CostEstimate(
            flops=12 * rows * width * 8 * width, bytes_accessed=32 * rows * width, transcendentals=0
        ),
    )(place, own, *operands)


def update_kernel(count, place, block, high, low, *refs):
    blocks, out, token, joined = refs[: 8 * count], refs[-4], refs[-3], refs[-2:]
    token[...] = jnp.zeros_like(token)
    each_pair(place, joined, blocks, count)
    tile = block.shape[0]
    rows = pl.ds(pl.multiple_of(pl.program_id(1) * tile, tile), tile)
    side = (joined[0][...], joined[1][...])
    out[...] = block[...] - product((high[rows], low[rows]), side, BOTH_LAST)


def update_step(place, matrix, slots, sides, blocks, before):
    rows = matrix.shape[0]
    depth, width = blocks[0].shape
    tile, count, start = rows // 2, len(slots), slots[0]
    block = pl.BlockSpec(
        (tile, 2 * depth),
        lambda pair, step, place: (step, (place[0] ^ (start + 2 * pair)) // 2),
    )
    operands = [matrix, *sides, *blocks]
    specs = [block] + [whole(operand.shape) for operand in operands[1:]]
    aliases = {}
    if before is not None:
        aliases = {1 + len(operands): 0}
        operands.append(before[0])
        specs.append(pl.BlockSpec(memory_space=pl.ANY))
    return pl.pallas_call(
        functools.partial(update_kernel, count),
        grid_spec=pltpu.PrefetchScalarGridSpec(
            num_scalar_prefetch=1,
            grid=(count, 2),
            in_specs=specs,
            out_specs=[block, whole((8, 128))],
            scratch_shapes=[pltpu.VMEM((2 * depth, 4 * width), BF16)] * 2,
        ),
        out_shape=[
            jax.ShapeDtypeStruct(matrix.shape, F32),
            jax.ShapeDtypeStruct((8, 128), jnp.int32),
        ],
        input_output_aliases=aliases,
        compiler_params=pltpu.CompilerParams(vmem_limit_bytes=VMEM_BYTES),
        cost_estimate=pl.CostEstimate(
            flops=6 * rows * depth * 8 * width * count,
            bytes_accessed=16 * rows * depth * count,
            transcendentals=0,
        ),
    )(place, *operands)


def steer(values, cost):
    anywhere = pl.BlockSpec(memory_space=pl.ANY)
    return pl.pallas_call(
        lambda *refs: None,
        in_specs=[anywhere] * len(values),
        out_specs=[anywhere] * len(values),
        out_shape=[jax.ShapeDtypeStruct(part.shape, part.dtype) for part in values],
        input_output_aliases={n: n for n in range(len(values))},
        cost_estimate=pl.CostEstimate(flops=int(cost * 1e9), bytes_accessed=0, transcendentals=0),
    )(*values)


def after(token, values):
    return jnp.where(token[0, 0] != 0, jnp.zeros_like(values), values)


def solution(mesh):
    row_count, col_count = mesh.shape["row"], mesh.shape["col"]
    group = row_count // col_count
    everyone = row_count * col_count
    assert group * col_count == row_count and group >= 4 and everyone & (everyone - 1) == 0
    halves = col_count == 2

    def flip(values, mask):
        return lax.ppermute(values, ("row", "col"), [(n, n ^ mask) for n in range(everyone)])

    def flip_row(values, mask):
        return flip(values, mask * col_count)

    def transpose(values, turn):
        pairs = []
        for s in range(col_count):
            for b in range(group):
                for j in range(col_count):
                    source = (s * group + b) * col_count + j
                    pairs.append((source, ((j - turn) % col_count * group + b) * col_count + s))
        return lax.ppermute(values, ("row", "col"), pairs)

    def spread(own, work, stages, gates):
        found = {0: own}

        def swapped(d, token=None):
            gone = found[d] if token is None else [after(token, part) for part in found[d]]
            return [part for n in range(2) for part in (found[d][n], flip_row(gone[n], 1))]

        if group == 8:
            ahead = flip_row(own[1], 2), flip_row(own[0], 4)
            behind = flip_row(own[0], 2), flip_row(own[1], 4)
            found[2], found[4] = [behind[0], ahead[0]], [ahead[1], behind[1]]
            token = None
            for number, slots in enumerate(stages):
                if 6 in slots:
                    if 6 not in found:
                        found[6] = [flip_row(ahead[1], 2), flip_row(ahead[0], 4)]
                    blocks = [swapped(d, token if gates[1] and d == 6 else None) for d in slots]
                else:
                    blocks = [swapped(d) for d in slots]
                token = work(slots, blocks)
                if number == 0 and gates[0]:
                    gone = [after(token, part) for part in ahead]
                    found[6] = [flip_row(gone[1], 2), flip_row(gone[0], 4)]
            return
        for d in range(2, group, 2):
            found[d] = [flip_row(part, d) for part in own]
        for d in range(0, group, 2):
            work((d,), [swapped(d)])

    def shards(matrix, panels, factors):
        row, col = lax.axis_index("row"), lax.axis_index("col")
        zero = jnp.zeros_like(row)
        place = jnp.stack(
            [row % group, col if halves else zero, row // group if halves else zero]
        ).astype(jnp.int32)
        vectors, sums, outs = {}, [None], [None]

        def forward(slots, blocks):
            vectors.update(zip(slots, blocks))
            sums[0] = forward_step(
                place,
                matrix,
                slots,
                sum(blocks, []),
                panels,
                sums[0],
                slots[-1] + 2 == group,
                1 / col_count,
            )
            return sums[0][1]

        spread([transpose(panels[0], 0), transpose(panels[1], 1)], forward, FORWARD, GATES[:2])
        kept, sent, inner = sums[0]
        if halves:
            mine = kept + flip(sent, 1)
            other = flip(mine, 1)
            blocks = [transpose(mine, 0), transpose(mine, 1)]
        else:
            mine, other = lax.psum((kept, sent), "col")
            blocks = [transpose(mine, 0), transpose(other, 1)]
        blocks = steer(blocks, 40)
        odd = row % 2 != 0
        upper, lower = inner[:2], inner[2:]
        part = jnp.where(odd, lower, upper) + flip_row(jnp.where(odd, upper, lower), 1)
        masks = [1 << n for n in range(everyone.bit_length() - 1) if 1 << n != col_count]
        for mask in masks:
            part = part + flip(part, mask)
        there = flip_row(part, 1)
        inner = jnp.concatenate([jnp.where(odd, there, part), jnp.where(odd, part, there)], axis=0)
        sides = mix(place, panels, mine, other, inner, factors)

        def update(slots, blocks):
            pairs = sum([block + vectors[slot] for slot, block in zip(slots, blocks)], [])
            outs[0] = update_step(place, matrix, slots, sides, pairs, outs[0])
            return outs[0][1]

        spread(blocks, update, UPDATE, GATES[2:])
        return outs[0][0]

    placed = (P("row", "col"), P(None, "row", None), P())
    return jax.shard_map(
        shards, mesh=mesh, in_specs=placed, out_specs=P("row", "col"), check_vma=False
    )
```
